32 devices in a mesh: row: 4 (over x, core), col: 8 (over z, y).
Axes of the slice: x: 2, y: 2, z: 4, core: 2. Of those that a mesh axis runs over, the one named last changes fastest.
Arguments:
- vectors: bfloat16 [16, 32768], P(None, ('row', 'col')), may hold values from -6 to 6
- tiles: bfloat16 [4, 8, 8, 512, 512], P('row', 'col'), may hold values from -0.25 to 0.25
- block_rows: int32 [4, 8, 8], P('row', 'col'), may hold values from 0 to 15
- block_cols: int32 [4, 8, 8], P('row', 'col'), may hold values from 0 to 7
- counts: int32 [4, 8], P('row', 'col'), may hold values from 1 to 8, as said below
Outputs:
- hx: float32 [16, 32768], P(None, ('row', 'col'))
The draws below stay inside these ranges and needn't reach their ends.
Inputs may be any that keep to these rules, and one draw needn't show every extreme that they name: `counts`: every tile has between 1 and 8 live blocks; in every draw one tile has all 8 slots live, the others at most half.
All inputs are finite; a program needn't handle non-finite values.
Results may differ from the reference program's by a relative error of at most 0.0003.
Values may be sent and summed in bfloat16 or wider, within the bound.
No kernel may reach another device: no remote copies, remote signals or barrier semaphores. Data moves between devices by JAX's collectives and lax.ppermute only.
A program may use at most 64 MiB of HBM per device.

```python
import jax
import jax.numpy as jnp
from jax import lax

VECS = 16
BLK = 512
BD = 2
NNZ_DEV = 8
ROWS = 32768
N_ROW = 4
N_COL = 8


def draw_counts(key, part):
    key = jax.random.fold_in(key, 7)
    first, second = jax.random.split(key)
    total = N_ROW * N_COL
    base = jax.random.randint(first, (total,), 1, NNZ_DEV // 2 + 1)
    chosen = jax.random.randint(second, (), 0, total)
    base = jnp.where(jnp.arange(total) == chosen, NNZ_DEV, base)
    return base.reshape(N_ROW, N_COL).astype(jnp.int32)


def plant(values, key, smallest, top_value):
    longest = values.shape.index(max(values.shape))
    spots = []
    for shift in (0, 1):
        where = [jax.random.randint(jax.random.fold_in(key, axis), (), 0, length) for axis, length in enumerate(values.shape)]
        where[longest] = (where[longest] + shift) % values.shape[longest]
        spots.append(tuple(where))
    return values.at[spots[0]].set(smallest).at[spots[1]].set(top_value)


def levels(key, dims, shards, smallest, high):
    def one(dim, shards_of):
        steps = jax.random.uniform(jax.random.fold_in(jax.random.fold_in(key, 6), dim), (shards_of,), jnp.float32, smallest / len(shards), high / len(shards))
        return jnp.repeat(jnp.exp(steps), dims[dim] // shards_of).reshape((-1,) + (1,) * (len(dims) - dim - 1))

    factor_of = one(*shards[0])
    for cut in shards[1:]:
        factor_of = factor_of * one(*cut)
    return factor_of


def centred(stream_key, extent, scale, most, pieces=(), held_as=jnp.bfloat16):
    values = jax.random.normal(stream_key, extent, jnp.float32) * scale
    if len(pieces) > 0:
        values = levels(stream_key, extent, pieces, -0.22, 0.18) * values
    return jnp.clip(values, min=-most, max=most).astype(held_as)


def setup_inputs(seed: int = 0) -> dict:
    seeds = jax.random.split(jax.random.key(seed), 6)
    vectors = centred(seeds[0], (VECS, ROWS), 1.0, 6.0, ((1, 32),))
    tiles = centred(seeds[1], (N_ROW, N_COL, NNZ_DEV, BLK, BLK), BLK ** -0.5, 0.25, ((0, 4), (1, 8)))
    block_rows = plant(jax.random.randint(seeds[2], (N_ROW, N_COL, NNZ_DEV), 0, N_COL * BD), jax.random.fold_in(seeds[2], 1), 0, (N_COL * BD) - 1).astype(jnp.int32)
    block_cols = plant(jax.random.randint(seeds[3], (N_ROW, N_COL, NNZ_DEV), 0, N_ROW * BD), jax.random.fold_in(seeds[3], 1), 0, (N_ROW * BD) - 1).astype(jnp.int32)
    counts = draw_counts(jax.random.fold_in(seeds[5], 71), 0)
    return dict(vectors=vectors, tiles=tiles, block_rows=block_rows, block_cols=block_cols, counts=counts)


def add_at(total, piece, start):
    width = piece.shape[1]
    old = lax.dynamic_slice_in_dim(total, start, width, 1)
    return lax.dynamic_update_slice_in_dim(total, old + piece, start, 1)


def reference(vectors, tiles, block_rows, block_cols, counts):
    block_size = tiles.shape[-1]
    group = N_COL * BD
    flat_tiles = tiles.reshape(N_ROW * N_COL * NNZ_DEV, block_size, block_size)
    row_ids = jnp.arange(N_ROW, dtype=jnp.int32)[:, None, None]
    col_ids = jnp.arange(N_COL, dtype=jnp.int32)[None, :, None]
    slot_ids = jnp.arange(NNZ_DEV, dtype=jnp.int32)[None, None, :]
    global_rows = (row_ids * group + block_rows).astype(jnp.int32).reshape(-1)
    global_cols = ((block_cols // BD) * group + col_ids * BD + block_cols % BD).astype(jnp.int32).reshape(-1)
    live = (slot_ids < counts[:, :, None]).reshape(-1)

    def apply_block(result, items):
        block, row_block, col_block, alive = items
        row_start = (row_block * block_size).astype(jnp.int32)
        col_start = (col_block * block_size).astype(jnp.int32)
        col_piece = lax.dynamic_slice_in_dim(vectors, col_start, block_size, 1)
        row_piece = lax.dynamic_slice_in_dim(vectors, row_start, block_size, 1)
        direct = lax.dot_general(col_piece, block, (((1,), (1,)), ((), ())), preferred_element_type=jnp.float32)
        mirror = jnp.dot(row_piece, block, preferred_element_type=jnp.float32)
        direct = jnp.where(alive, direct, jnp.zeros_like(direct))
        mirror = jnp.where(alive, mirror, jnp.zeros_like(mirror))
        result = add_at(result, direct, row_start)
        result = add_at(result, mirror, col_start)
        return result, None

    result = jnp.zeros((vectors.shape[0], vectors.shape[1]), jnp.float32)
    result, _ = lax.scan(apply_block, result, (flat_tiles, global_rows, global_cols, live))
    return result
```

```python
import functools

import jax
import jax.numpy as jnp
from jax import lax
from jax.experimental import pallas as pl
from jax.experimental.pallas import tpu as pltpu
from jax.sharding import PartitionSpec as P

F32 = jnp.float32
I16 = jnp.int16
LANES = 128
STEPS = 64.0
TOP = 32700.0
VMEM = pl.BlockSpec(memory_space=pltpu.VMEM)
SMEM = pl.BlockSpec(memory_space=pltpu.SMEM)
ANY = pl.BlockSpec(memory_space=pl.ANY)


def coded(total):
    biggest = jnp.max(jnp.abs(total), axis=1, keepdims=True)
    code = jnp.ceil(STEPS * jnp.log2(jnp.maximum(biggest, 2.0 ** -126)))
    scaled = total * jnp.exp2(code * (-1.0 / STEPS))
    return jnp.floor(scaled * TOP + 0.5).astype(jnp.int32).astype(I16), code


def write_piece(piece, totals):
    size, depth = totals[0].shape[1], len(totals)
    spot = lax.broadcasted_iota(jnp.int32, (totals[0].shape[0], LANES), 1)
    codes = jnp.zeros(spot.shape, F32)
    for k, total in enumerate(totals):
        values, code = coded(total)
        piece[:, k * size:(k + 1) * size] = values
        codes = jnp.where(spot >= k * (LANES // depth), code, codes)
    piece[:, depth * size:] = codes.astype(jnp.int32).astype(I16)


def read_piece(piece, depth):
    size = (piece.shape[1] - LANES) // depth
    codes = piece[:, depth * size:].astype(jnp.int32).astype(F32)
    scales = jnp.exp2(codes * (1.0 / STEPS)) * (1.0 / TOP)
    parts = []
    for k in range(depth):
        spot = k * (LANES // depth)
        part = piece[:, k * size:(k + 1) * size].astype(jnp.int32).astype(F32)
        parts.append(part * scales[:, spot:spot + 1])
    return parts


def mark(out):
    out[...] = jnp.zeros_like(out)


def stack_pieces(n_pieces, *refs):
    stack = refs[-1]
    for d, piece in enumerate(refs[:n_pieces][::-1]):
        stack[d] = piece[...]


def gathered_place(block, depth, me, size, nears, odd):
    apart, places = lax.bitwise_xor(block // depth, me), []
    for near in nears:
        at_far = apart % near + apart // (2 * near) * near
        places.append((apart // near % 2 * (size // 2) + at_far) * depth + block % depth)
    return jnp.where(odd, places[1], places[0])


def turned(distance, odd):
    low = 2 if odd else 1
    bits = distance // low % 2, distance // (2 * low) % 2
    return distance + (bits[1] - bits[0]) * low + (bits[0] - bits[1]) * 2 * low


def summed_place(apart, block, depth, n_far, part):
    return (apart % part * n_far + apart // part) * depth + block % depth


def load_pieces(x, *stacks):
    size, at = x.shape[2], 0
    for stack in stacks:
        for d in range(stack.shape[0]):
            for k in range(stack.shape[2] // size):
                x[at] = stack[d, :, k * size:(k + 1) * size]
                at += 1


def store_pieces(total, kept, *leaving):
    n_far, size = kept.shape[0], total.shape[2]
    depth = kept.shape[2] // size
    for d in range(n_far):
        for a, out in enumerate(leaving):
            at = ((len(leaving) - a) * n_far + d) * depth
            write_piece(out.at[d], [total[at + k] for k in range(depth)])
        for k in range(depth):
            kept[d, :, k * size:(k + 1) * size] = total[d * depth + k]


def work_blocks(index_ref, count_ref, held, x, total, find, contract):
    slots = held.shape[0]
    group = slots // 2 if slots % 2 == 0 else slots
    count = count_ref[0, 0]

    def work(at):
        parts = []
        for slot in range(at, at + group):
            source, target = find(index_ref[slot], index_ref[slots + slot])
            product = lax.dot_general(
                x[source], held[slot], (((1,), (contract,)), ((), ())), preferred_element_type=F32
            )
            parts.append((target, jnp.where(slot < count, product, 0.0)))
        for target, product in parts:
            total[target] += product

    total[...] = jnp.zeros_like(total)
    for at in range(0, slots, group):
        @pl.when(at < count)
        def _():
            work(at)


def direct_blocks(plan, index_ref, count_ref, tiles, *refs):
    pieces, (kept, *leaving), (x, total) = refs[:2], refs[2:-2], refs[-2:]
    held, depth = tiles.at[0, 0], kept.shape[2] // tiles.shape[-1]
    row_me, col_me = lax.axis_index("row"), lax.axis_index("col")
    odd = row_me % 2 == 1

    def find(p, q):
        apart = lax.bitwise_xor(p // depth, col_me)
        apart = jnp.where(odd, turned(apart, True), turned(apart, False))
        return (
            gathered_place(q, depth, row_me, x.shape[0] // depth, plan["row"][0], odd),
            summed_place(apart, p, depth, kept.shape[0], plan["col"][1]),
        )

    load_pieces(x, *pieces)
    work_blocks(index_ref, count_ref, held, x, total, find, 1)
    store_pieces(total, kept, *leaving)


def mirror_blocks(plan, index_ref, count_ref, tiles, *refs):
    pieces, (kept, *leaving), (x, total) = refs[:2], refs[3:-2], refs[-2:]
    held, depth = tiles.at[0, 0], kept.shape[2] // tiles.shape[-1]
    row_me, col_me = lax.axis_index("row"), lax.axis_index("col")
    odd = row_me % 2 == 1

    def find(p, q):
        apart = lax.bitwise_xor(q // depth, row_me)
        return (
            gathered_place(p, depth, col_me, x.shape[0] // depth, plan["col"][0], odd),
            summed_place(apart, q, depth, kept.shape[0], plan["row"][1]),
        )

    load_pieces(x, *pieces)
    work_blocks(index_ref, count_ref, held, x, total, find, 0)
    store_pieces(total, kept, *leaving)


def add_near(depth, kept, *refs):
    n_far = kept.shape[0]
    came, late, (mine, *far_out), late_out = refs[:-n_far - 2], refs[-n_far - 2], refs[-n_far - 1:-1], refs[-1]
    size = mine.shape[2] // depth
    cuts = [slice(k * size, (k + 1) * size) for k in range(depth)]
    for d in range(n_far):
        totals = [kept[d, :, cut] for cut in cuts]
        for piece in came:
            totals = [total + part for total, part in zip(totals, read_piece(piece.at[d], depth))]
        if d > 0:
            write_piece(far_out[d - 1].at[0], totals)
            continue
        for cut, total in zip(cuts, totals):
            mine[0, :, cut] = total
    late_out[...] = late[...]


def add_up(depth, n_sums, *refs):
    sums, came, result = refs[:n_sums], refs[n_sums:-1], refs[-1]
    size = result.shape[1] // depth
    cuts = [slice(k * size, (k + 1) * size) for k in range(depth)]
    totals = [sum(part[0, :, cut] for part in sums) for cut in cuts]
    for piece in came:
        totals = [total + part for total, part in zip(totals, read_piece(piece.at[0], depth))]
    for cut, total in zip(cuts, totals):
        result[:, cut] = total


def on_device(n_row, n_col, vectors, tiles, block_rows, block_cols, counts):
    vecs, width = vectors.shape
    slots, size = tiles.shape[2], tiles.shape[-1]
    depth = width // size
    sizes = {"row": n_row, "col": n_col}
    plan = {"row": ((1, 1), 4), "col": ((2, 1), 4)}
    far = {axis: n // plan[axis][1] for axis, n in sizes.items()}
    piece = jax.ShapeDtypeStruct((vecs, width + LANES), I16)
    whole = jax.ShapeDtypeStruct((vecs, width), F32)

    def many(n, one):
        return jax.ShapeDtypeStruct((n,) + one.shape, one.dtype)

    def swap(value, axis, apart):
        pairs = []
        for r in range(n_row):
            for c in range(n_col):
                to = (r ^ apart[r % 2], c) if axis == "row" else (r, c ^ apart[r % 2])
                pairs.append((r * n_col + c, to[0] * n_col + to[1]))
        return lax.ppermute(value, ("row", "col"), pairs)

    def gather_ways(axis):
        longest = range(sizes[axis] - 1, 0, -1)
        return list(zip(*([d for d in longest if not d & near] for near in plan[axis][0])))

    def ways(axis, distances):
        return [
            tuple(turned(d, odd) if axis == "col" else d for odd in (False, True)) for d in distances
        ]

    def near_ways(axis):
        return ways(axis, range(plan[axis][1] - 1, 0, -1))

    def far_ways(axis):
        part = plan[axis][1]
        return ways(axis, range(sizes[axis] - part, 0, -part))

    def small_call(body, outs, name, operands):
        total = sum(x.size * x.dtype.itemsize for x in list(outs) + list(operands))
        return pl.pallas_call(
            body,
            out_shape=outs,
            in_specs=[VMEM] * len(operands),
            out_specs=[VMEM] * len(outs),
            compiler_params=pltpu.CompilerParams(vmem_limit_bytes=2**21 + 2 * total),
            name=name,
        )(*operands)

    def block_call(body, axis_in, axis_out, pieces, name, after=()):
        return pl.pallas_call(
            functools.partial(body, plan),
            out_shape=[many(far[axis_out], whole)]
            + [many(far[axis_out], piece)] * (plan[axis_out][1] - 1),
            in_specs=[SMEM] * 2 + [VMEM] * 3 + [ANY] * len(after),
            out_specs=[VMEM] * plan[axis_out][1],
            scratch_shapes=[
                pltpu.VMEM((sizes[axis_in] * depth, vecs, size), vectors.dtype),
                pltpu.VMEM((sizes[axis_out] * depth, vecs, size), F32),
            ],
            compiler_params=pltpu.CompilerParams(vmem_limit_bytes=16 * 2**20),
            cost_estimate=pl.CostEstimate(
                flops=slots * 200 * vecs * size * size,
                bytes_accessed=slots * size * size * 16,
                transcendentals=0,
            ),
            name=name,
        )(index, counts, tiles, *pieces, *after)

    def stack(axis, *after):
        pieces = [got[axis, way] for way in gather_ways(axis)] + [vectors]
        body = functools.partial(stack_pieces, len(pieces))
        outs = [jax.ShapeDtypeStruct((len(pieces), vecs, width), vectors.dtype)]
        return small_call(body, outs, "stack_pieces", [*pieces, *after])[0]

    index = jnp.concatenate([block_rows[0, 0], block_cols[0, 0]])
    got = {
        (axis, way): swap(vectors, axis, way) for axis in ("row", "col") for way in gather_ways(axis)
    }
    marked = pl.pallas_call(
        mark,
        out_shape=jax.ShapeDtypeStruct((vecs, LANES), F32),
        out_specs=VMEM,
        compiler_params=pltpu.CompilerParams(vmem_limit_bytes=2**21),
        cost_estimate=pl.CostEstimate(
            flops=2 * 10**9, bytes_accessed=2**22, transcendentals=0
        ),
        name="mark",
    )()
    row_stack = stack("row", marked)
    row_pieces = [row_stack, swap(row_stack, "row", plan["row"][0])]
    col_kept, *leaving = block_call(direct_blocks, "row", "col", row_pieces, "direct_blocks")
    col_stack = stack("col", marked)
    col_pieces = [col_stack, swap(col_stack, "col", plan["col"][0])]
    col_came = [swap(out, "col", way) for out, way in zip(leaving, near_ways("col"))]
    row_kept, *leaving = block_call(
        mirror_blocks, "col", "row", col_pieces, "mirror_blocks", [col_kept]
    )
    *first, last = near_ways("row")
    row_came = [swap(out, "row", way) for out, way in zip(leaving, first)]

    col_kept, *far_out, late = small_call(
        functools.partial(add_near, depth),
        [many(1, whole)] + [many(1, piece)] * (far["col"] - 1) + [many(far["row"], piece)],
        "add_near",
        [col_kept, *col_came, leaving[-1]],
    )
    col_came = [swap(out, "col", way) for out, way in zip(far_out[::-1], far_ways("col"))]
    row_came.append(swap(late, "row", last))
    if far["row"] > 1:
        row_kept, *far_out, _ = small_call(
            functools.partial(add_near, depth),
            [many(1, whole)] + [many(1, piece)] * far["row"],
            "add_near",
            [row_kept, *row_came, col_came[0]],
        )
        row_came = [swap(out, "row", way) for out, way in zip(far_out[::-1], far_ways("row"))]
    sums = [col_kept, row_kept]
    body = functools.partial(add_up, depth, len(sums))
    return small_call(body, [whole], "add_up", [*sums, *col_came, *row_came])[0]


def solution(mesh):
    placed = (
        P(None, ("row", "col")),
        P("row", "col", None, None, None),
        P("row", "col", None),
        P("row", "col", None),
        P("row", "col"),
    )
    return jax.shard_map(
        functools.partial(on_device, mesh.shape["row"], mesh.shape["col"]),
        mesh=mesh,
        in_specs=placed,
        out_specs=P(None, ("row", "col")),
        check_vma=False,
    )
```
